32 devices in a mesh: groups: 2 (over x), dp: 16 (over z, y, core).
Axes of the slice: x: 2, y: 2, z: 4, core: 2. Of those that a mesh axis runs over, the one named last changes fastest.
Arguments:
- latents: bfloat16 [320, 8, 8, 640], P(('groups', 'dp')), parts along dimension 0, may hold values from -6 to 6
- targets: bfloat16 [320, 8, 8, 320], P(('groups', 'dp')), parts along dimension 0, may hold values from -6 to 6
- heights: int32 [320], P('groups'), parts along dimension 0, may hold values from 4 to 8
- widths: int32 [320], P('groups'), parts along dimension 0, may hold values from 4 to 8
- owner: int32 [320], P('groups'), parts along dimension 0, may hold values from -1 to 15, as said below
- weight: bfloat16 [5760, 320], P('dp'), may hold values from -0.078125 to 0.078125
- probe: bfloat16 [11520, 320], P(('groups', 'dp')), parts along dimension 0, may hold values from -0.078125 to 0.078125
Outputs:
- hvp: float32 [11520, 320], P(('groups', 'dp')), parts along dimension 0
The draws below stay inside these ranges and needn't reach their ends.
There are 2 independent parts, one for each index of `groups`. The reference program is written for one: setup_inputs(seed, part) draws one part's arguments, and reference() takes and returns one part's arrays. A program takes and returns all parts, laid end to end along the dimension named above; an argument that names none is the same for every part. Nothing has to cross between parts.
Inputs may be any that keep to these rules, and one draw needn't show every extreme that they name: Slot s lies on device s // 10 of dp. owner[s] is -1 for an empty slot, else that device or its partner, the device whose index differs in the lowest bit. Every device owns exactly 5 samples. In every draw some device holds 10 filled slots, 5 of them owned by its partner.
All inputs are finite; a program needn't handle non-finite values.
Results may differ from the reference program's by a relative error of at most 0.0039.
Values may be sent and summed in bfloat16 or wider, within the bound.
A program may use at most 64 MiB of HBM per device.

```python
import jax
import jax.numpy as jnp
from jax import lax

CHANNELS = 640
OUT_CHANNELS = 320
GROUPS = 32
OWNED_SAMPLES = 5
FRAME_ROWS = 8
FRAME_COLS = 8
KERNEL_ROWS = 5760
ALL_SLOTS = 160
N_DP = 16


def draw_owner(key, part):
    pair_count = N_DP // 2
    key_side, key_surplus, key_forced, key_rank = jax.random.split(jax.random.fold_in(key, 7), 4)
    heavy_pick = jax.random.randint(key_side, (pair_count,), 0, 2)
    surplus = jax.random.randint(key_surplus, (pair_count,), 0, OWNED_SAMPLES + 1)
    forced = jax.random.randint(key_forced, (), 0, pair_count)
    surplus = jnp.where(jnp.arange(pair_count) == forced, OWNED_SAMPLES, surplus)
    device = jnp.arange(N_DP, dtype=jnp.int32)
    is_heavy = device % 2 == heavy_pick[device // 2]
    filled = jnp.where(is_heavy, OWNED_SAMPLES + surplus[device // 2], OWNED_SAMPLES - surplus[device // 2])
    ranking = jax.vmap(lambda sub_key: jax.random.permutation(sub_key, 2 * OWNED_SAMPLES))(jax.random.split(key_rank, N_DP))
    partner = jnp.bitwise_xor(device, 1)
    stays_home = (ranking < OWNED_SAMPLES) | jnp.logical_not(is_heavy)[:, None]
    destination = jnp.where(stays_home, device[:, None], partner[:, None])
    result = jnp.where(ranking < filled[:, None], destination, -1)
    return result.reshape(2 * OWNED_SAMPLES * N_DP).astype(jnp.int32)


def touch_ends(values, stream_key, smallest, high):
    shape = values.shape
    index_at = [jax.random.randint(jax.random.fold_in(stream_key, axis), (), 0, shape[axis]) for axis in range(len(shape))]
    values = values.at[tuple(index_at)].set(smallest)
    longest = shape.index(max(shape))
    index_at[longest] = (index_at[longest] + 1) % shape[longest]
    return values.at[tuple(index_at)].set(high)


def spiked(array, key, source, target, shards_of, factor):
    owner, partner = [(jnp.arange(array.shape[dim]) // (array.shape[dim] // shards_of)).reshape([-1 if axis == dim else 1 for axis in range(array.ndim)]) for dim in (source, target)]
    chosen = jax.random.permutation(key, shards_of)[partner]
    strong = (owner == chosen) | (owner == (partner + shards_of // 2) % shards_of)
    return jnp.where(strong, factor * array, array)


def levels(own_key, shape, shards, low, high):
    level, own = 1.0, jax.random.fold_in(own_key, 6)
    for axis_at, shards_of in shards:
        steps = jnp.exp(jax.random.uniform(jax.random.fold_in(own, axis_at), (shards_of,), jnp.float32, low / len(shards), high / len(shards)))
        level = level * jnp.repeat(steps, shape[axis_at] // shards_of).reshape([-1 if axis == axis_at else 1 for axis in range(len(shape))])
    return level


def normal_values(key, dims, scale, bound, cuts=(), held_as=jnp.bfloat16):
    array = jax.random.normal(key, dims, jnp.float32) * scale
    if len(cuts) > 0:
        array = levels(key, dims, cuts, -0.22, 0.18) * array
    return jnp.clip(array, min=-bound, max=bound).astype(held_as)


def noise_with(key, shape, scale, bound, pieces, heavy, kind=jnp.bfloat16):
    values = scale * jax.random.normal(key, shape, jnp.float32)
    if pieces:
        values = values * levels(key, shape, pieces, -0.22, 0.18)
    return jnp.clip(spiked(values, jax.random.fold_in(key, 3), *heavy), -bound, bound).astype(kind)


def setup_inputs(seed: int = 0, part: int = 0) -> dict:
    streams_of = jax.random.split(jax.random.key(seed), 8)
    part_keys = jax.random.split(jax.random.fold_in(streams_of[7], part), 8)
    latents = noise_with(part_keys[0], (ALL_SLOTS, FRAME_ROWS, FRAME_COLS, CHANNELS), 1.0, 6.0, ((0, 16),), (0, 3, 16, 2.0))
    targets = normal_values(part_keys[1], (ALL_SLOTS, FRAME_ROWS, FRAME_COLS, OUT_CHANNELS), 1.0, 6.0, ((0, 16),))
    heights = touch_ends(jax.random.randint(part_keys[2], (ALL_SLOTS,), FRAME_ROWS // 2, FRAME_ROWS + 1), jax.random.fold_in(part_keys[2], 1), FRAME_ROWS // 2, FRAME_ROWS).astype(jnp.int32)
    widths = touch_ends(jax.random.randint(part_keys[3], (ALL_SLOTS,), FRAME_COLS // 2, FRAME_COLS + 1), jax.random.fold_in(part_keys[3], 1), FRAME_COLS // 2, FRAME_COLS).astype(jnp.int32)
    owner = draw_owner(jax.random.fold_in(jax.random.fold_in(streams_of[7], part), 71), part)
    weight = normal_values(streams_of[5], (KERNEL_ROWS, OUT_CHANNELS), KERNEL_ROWS ** -0.5, 0.078125, ((0, 16),))
    probe = normal_values(part_keys[6], (KERNEL_ROWS, OUT_CHANNELS), KERNEL_ROWS ** -0.5, 0.078125, ((0, 16),))
    return dict(latents=latents, targets=targets, heights=heights, widths=widths, owner=owner, weight=weight, probe=probe)


EPSILON = 1e-05

def group_onehot(channels):
    per_group = CHANNELS // GROUPS
    group_count = channels // per_group
    return (jnp.arange(channels)[:, None] // per_group == jnp.arange(group_count)[None, :]).astype(jnp.float32)

def group_norm(values, spatial):
    channels = values.shape[-1]
    onehot = group_onehot(channels)
    highest = lax.Precision.HIGHEST
    pixel_weights = spatial[:, :, :, None]
    counts = lax.optimization_barrier(jnp.sum(spatial, axis=(1, 2))) * (CHANNELS // GROUPS)
    group_sums = jnp.dot(lax.optimization_barrier(jnp.sum(values * pixel_weights, axis=(1, 2))), onehot, precision=highest)
    channel_mean = jnp.dot(group_sums / counts[:, None], onehot.T, precision=highest)
    centred = values - channel_mean[:, None, None, :]
    group_squares = jnp.dot(lax.optimization_barrier(jnp.sum(centred * centred * pixel_weights, axis=(1, 2))), onehot, precision=highest)
    channel_scale = jnp.dot(lax.rsqrt(group_squares / counts[:, None] + EPSILON), onehot.T, precision=highest)
    return centred * channel_scale[:, None, None, :]

def frame_mask(heights, widths, frame_rows, frame_cols):
    inside_rows = jnp.arange(frame_rows, dtype=jnp.int32)[None, :] < heights[:, None]
    inside_cols = jnp.arange(frame_cols, dtype=jnp.int32)[None, :] < widths[:, None]
    return (inside_rows[:, :, None] & inside_cols[:, None, :]).astype(jnp.float32)

def unfold(hidden):
    samples, frame_rows, frame_cols, channels = hidden.shape
    padded = jnp.pad(hidden, ((0, 0), (1, 1), (1, 1), (0, 0)))
    shifted = [padded[:, offset_row:offset_row + frame_rows, offset_col:offset_col + frame_cols, :] for offset_row in range(3) for offset_col in range(3)]
    return jnp.concatenate(shifted, axis=-1).reshape(samples * frame_rows * frame_cols, 9 * channels)

def second_order(pre_norm, tangent, wanted, spatial, live_flag, factor):
    loss_weights = (spatial * live_flag[:, None, None])[:, :, :, None]

    def loss_value(values):
        activated = jax.nn.silu(group_norm(values, spatial))
        missing = activated - wanted
        return 0.5 * factor * jnp.sum(loss_weights * missing * missing)

    def along_tangent(values):
        return jnp.sum(jax.grad(loss_value)(values) * tangent)
    return jax.grad(along_tangent)(pre_norm)

def reference(latents, targets, heights, widths, owner, weight, probe):
    slot_count = latents.shape[0]
    position = jnp.arange(slot_count, dtype=jnp.int32)
    ordering = jnp.argsort(jnp.where(owner >= 0, position, position + slot_count)).astype(jnp.int32)
    live_total = OWNED_SAMPLES * N_DP
    block_size = OWNED_SAMPLES
    block_count = live_total // block_size
    chosen = ordering[:live_total].reshape(block_count, block_size)
    factor = 1.0 / live_total

    def accumulate(running, picked):
        frames = jnp.take(latents, picked, axis=0)
        wanted = jnp.take(targets, picked, axis=0).astype(jnp.float32)
        spatial = frame_mask(jnp.take(heights, picked), jnp.take(widths, picked), FRAME_ROWS, FRAME_COLS)
        live_flag = (jnp.take(owner, picked) >= 0).astype(jnp.float32)
        hidden = (jax.nn.silu(group_norm(frames.astype(jnp.float32), spatial)) * spatial[:, :, :, None]).astype(jnp.bfloat16)
        patches = unfold(hidden)
        field_shape = (block_size, FRAME_ROWS, FRAME_COLS, OUT_CHANNELS)
        forward = jnp.dot(patches, weight, preferred_element_type=jnp.float32).reshape(field_shape)
        tangent = jnp.dot(patches, probe, preferred_element_type=jnp.float32).reshape(field_shape)
        curvature = second_order(forward, tangent, wanted, spatial, live_flag, factor)
        curvature = curvature.astype(jnp.bfloat16).reshape(-1, OUT_CHANNELS)
        running = running + lax.dot_general(patches, curvature, (((0,), (0,)), ((), ())), preferred_element_type=jnp.float32)
        return (running, None)
    result, _ = lax.scan(accumulate, jnp.zeros((KERNEL_ROWS, OUT_CHANNELS), jnp.float32), chosen)
    return result
```

```python
import functools

import jax
import jax.numpy as jnp
from jax import lax
from jax.experimental import pallas as pl
from jax.experimental.pallas import tpu as pltpu
from jax.sharding import PartitionSpec as P

PER_GROUP = 20
EPSILON = 1e-05
BLOCK = 8
CHIPS = BLOCK // 2
CELLS = 64
LANES = 128
MESH = pl.DeviceIdType.MESH
F32 = jnp.float32
BF16 = jnp.bfloat16


def up(value, step):
    return -(-value // step) * step


def thirds(value):
    high = value.astype(BF16)
    rest = value - high.astype(F32)
    mid = rest.astype(BF16)
    low = (rest - mid.astype(F32)).astype(BF16)
    return high, mid, low


def times_onehot(value, onehot):
    rows = value.shape[0]
    stacked = jnp.concatenate(
        [part.astype(F32) for part in thirds(value)], axis=0
    ).astype(BF16)
    product = jnp.dot(stacked, onehot, preferred_element_type=F32)
    return product[:rows] + product[rows : 2 * rows] + product[2 * rows :]


def onehot_times(onehot, value):
    high, mid, low = thirds(value)
    dot = functools.partial(jnp.dot, preferred_element_type=F32)
    return dot(onehot, high) + dot(onehot, mid) + dot(onehot, low)


def between(inner, outer, width):
    return (inner >= outer * width) & (inner < outer * width + width)


def iota(shape, axis):
    return lax.broadcasted_iota(jnp.int32, shape, axis)


def window_of(start, width, total):
    size = min(up(width + LANES - 1, LANES), total)
    return min(start // LANES * LANES, total - size), size


def kernel(
    n, factor, pick, high, wide, lat_in, tgt_in, w_in, mask_in, out,
    lat, tgt, w_buf, w_flat, wall, hid, t_out, t_buf, z, u_buf, t_tan, curv, acc, r_out, r_buf,
    lat_send, lat_recv, tgt_send, tgt_recv, w_send, w_recv, h_send, h_recv, t_send, t_recv,
    r_send, r_recv,
):
    me = lax.axis_index("dp")
    pos = lax.rem(me, BLOCK)
    base = me - pos
    chip = pos // 2
    core = lax.rem(pos, 2)
    partner = me + 1 - 2 * core
    slots = lat_in.shape[0]
    owned = slots // 2
    pair = 2 * owned
    width = pair * CELLS
    half = owned * CELLS
    channels = lat_in.shape[2]
    rows = w_rows = out.shape[1]
    del w_rows
    cols = out.shape[0] // BLOCK
    kernel_rows = w_flat.shape[1]
    share = kernel_rows // n

    barrier = pltpu.get_barrier_semaphore()

    def greet(k, _):
        pl.semaphore_signal(
            barrier, inc=1, device_id={"dp": lax.rem(me + k, n)}, device_id_type=MESH
        )
        return 0

    lax.fori_loop(1, n, greet, 0)
    pl.semaphore_wait(barrier, n - 1)

    def remote(src, dst, send, recv, target):
        return pltpu.make_async_remote_copy(
            src_ref=src, dst_ref=dst, send_sem=send, recv_sem=recv,
            device_id={"dp": target}, device_id_type=MESH,
        )

    lat_copy = remote(lat_in, lat.at[core], lat_send, lat_recv, partner)
    lat_copy.start()
    tgt_copy = remote(tgt_in, tgt.at[core], tgt_send, tgt_recv, partner)
    tgt_copy.start()

    def send_w(k, _):
        target = lax.rem(me + k, n)
        remote(w_in.at[lax.rem(target, BLOCK)], w_buf.at[me], w_send, w_recv, target).start()
        return 0

    lax.fori_loop(1, n, send_w, 0)
    w_own = pltpu.make_async_copy(w_in.at[pos], w_buf.at[me], w_recv)
    w_own.start()
    lat[core] = lat_in[...]
    tgt[core] = tgt_in[...]
    lat_copy.wait_recv()

    to_group = between(
        iota((channels, LANES), 0), iota((channels, LANES), 1), PER_GROUP
    ).astype(F32).astype(BF16)
    from_group = between(
        iota((LANES, channels), 1), iota((LANES, channels), 0), PER_GROUP
    ).astype(F32).astype(BF16)
    cell = iota((CELLS, channels), 0)
    cell_row, cell_col = cell >> 3, cell & 7
    frames, inside, counts = [], [], []
    for k in range(owned):
        which = pick[core * owned + k]
        tall, broad = high[core * owned + k], wide[core * owned + k]
        frames.append(lat[which // slots, lax.rem(which, slots)].astype(F32))
        inside.append(((cell_row < tall) & (cell_col < broad)).astype(F32))
        counts.append(jnp.full((1, LANES), tall * broad * PER_GROUP, jnp.int32).astype(F32))
    spare = 8 - owned
    counts = jnp.concatenate(counts + [jnp.ones((spare, LANES), F32)], axis=0)

    def group_mean(values):
        sums = [jnp.sum(v * m, axis=0, keepdims=True) for v, m in zip(values, inside)]
        sums = jnp.concatenate(sums + [jnp.zeros((spare, channels), F32)], axis=0)
        return times_onehot(sums, to_group) / counts

    mean = times_onehot(group_mean(frames), from_group)
    centred = [v - mean[k : k + 1] for k, v in enumerate(frames)]
    square = group_mean([v * v for v in centred])
    scale = times_onehot(lax.rsqrt(square + EPSILON), from_group)
    for k in range(owned):
        x = centred[k] * scale[k : k + 1]
        hid[pos, k * CELLS : (k + 1) * CELLS] = (
            x / (1.0 + jnp.exp(-x)) * inside[k]
        ).astype(BF16)

    def send_hidden(k, _):
        target = base + lax.rem(pos + k, BLOCK)
        remote(hid.at[pos], hid.at[pos], h_send, h_recv, target).start()
        return 0

    lax.fori_loop(1, BLOCK, send_hidden, 0)

    tgt_copy.wait_recv()
    chosen = []
    for k in range(pair):
        which = pick[k]
        chosen.append(tgt[which // slots, lax.rem(which, slots)].astype(F32))
    turned = jnp.concatenate(chosen, axis=0).T
    t_rows = t_out.shape[1]
    for b in range(BLOCK):
        t_out[b] = jnp.concatenate(
            [turned[b * cols : (b + 1) * cols], jnp.zeros((t_rows - cols, width), F32)], axis=0
        ).astype(BF16)
    t_buf[chip] = t_out[pos]

    def send_targets(k, _):
        there = 2 * lax.rem(chip + k, CHIPS) + core
        remote(t_out.at[there], t_buf.at[chip], t_send, t_recv, base + there).start()
        return 0

    lax.fori_loop(1, CHIPS, send_targets, 0)

    remote(w_buf, w_buf, w_send, w_recv, partner).wait_recv()
    w_flat[...] = jnp.zeros_like(w_flat)
    for d in range(n):
        start, size = window_of(d * share, share, kernel_rows)
        piece = w_buf[d].astype(F32)
        lane = iota(piece.shape, 1)
        piece = jnp.where(lane < share, piece, 0.0)
        if size > rows:
            piece = jnp.concatenate(
                [piece, jnp.zeros((piece.shape[0], size - rows), F32)], axis=1
            )
        if d * share > start:
            piece = pltpu.roll(piece, d * share - start, 1)
        w_flat[:, start : start + size] += piece
    both = 2 * cols
    for tap in range(9):
        wall[tap * both : (tap + 1) * both] = w_flat[
            :, tap * channels : (tap + 1) * channels
        ].astype(BF16)

    lane = iota((1, width), 1)
    lane_row, lane_col = (lane >> 3) & 7, lane & 7

    def tap_of(tap):
        a, b = tap // 3 - 1, tap % 3 - 1
        valid = (
            (lane_row + a >= 0) & (lane_row + a < 8) & (lane_col + b >= 0) & (lane_col + b < 8)
        )
        return a * 8 + b, valid.astype(F32)

    remote(
        hid.at[pl.ds(0, BLOCK - 1)], hid.at[pl.ds(0, BLOCK - 1)], h_send, h_recv, partner
    ).wait_recv()

    def forward(q, _):
        features = hid[pl.ds(2 * q, 2)].reshape(width, channels)
        z[...] = lax.dot_general(
            wall[...], features, (((1,), (1,)), ((), ())), preferred_element_type=F32
        )
        total = z[4 * both : 5 * both]
        for tap in range(9):
            if tap != 4:
                offset, valid = tap_of(tap)
                total = total + valid * pltpu.roll(
                    z[tap * both : (tap + 1) * both], -offset % width, 1
                )
        u_buf[q] = total[:cols]
        t_tan[q] = total[cols:]
        return 0

    lax.fori_loop(0, CHIPS, forward, 0)
    remote(
        t_buf.at[pl.ds(0, CHIPS - 1)], t_buf.at[pl.ds(0, CHIPS - 1)], t_send, t_recv, partner
    ).wait_recv()

    wide_rows = CHIPS * cols
    to_sample = between(
        iota((width, LANES), 0), iota((width, LANES), 1), CELLS
    ).astype(F32).astype(BF16)
    from_sample = between(
        iota((LANES, width), 1), iota((LANES, width), 0), CELLS
    ).astype(F32).astype(BF16)
    row, col = iota((wide_rows, LANES), 0), iota((wide_rows, LANES), 1)
    to_norm = between(row, col, PER_GROUP).astype(F32).astype(BF16)
    row, col = iota((LANES, wide_rows), 1), iota((LANES, wide_rows), 0)
    of_norm = between(row, col, PER_GROUP).astype(F32).astype(BF16)
    mask = jnp.concatenate(
        [jnp.broadcast_to(mask_in[q, 0:1], (cols, width)) for q in range(CHIPS)], axis=0
    )
    per_sample = jnp.dot(mask.astype(BF16), to_sample, preferred_element_type=F32)
    inverse = 1.0 / (jnp.maximum(per_sample, 1.0) * PER_GROUP)

    def small(value):
        return onehot_times(to_norm, onehot_times(of_norm, times_onehot(value, to_sample))) * inverse

    def spread(value):
        return times_onehot(value, from_sample)

    u = u_buf[...].reshape(wide_rows, width)
    t = t_tan[...].reshape(wide_rows, width)
    c = u - spread(small(u * mask))
    r = spread(lax.rsqrt(small(c * c * mask) + EPSILON))
    x = c * r
    wanted = jnp.concatenate([t_buf[q].astype(F32)[:cols] for q in range(CHIPS)], axis=0)
    a = spread(small(x * t * mask))
    x_dot = r * (t - spread(small(t * mask)) - x * a)
    sigma = 1.0 / (1.0 + jnp.exp(-x))
    missing = x * sigma - wanted
    first = sigma * (1.0 + x * (1.0 - sigma))
    second = sigma * (1.0 - sigma) * (2.0 + x * (1.0 - 2.0 * sigma))
    weight = factor * mask
    g = weight * missing * first
    g_dot = weight * (first * first + missing * second) * x_dot
    b = spread(small(g * x))
    h = g - spread(small(g)) - x * b
    h_dot = g_dot - spread(small(g_dot)) - x_dot * b - x * spread(small(g_dot * x + g * x_dot))
    result = mask * (r * h_dot - r * r * a * h)
    curv[...] = result.reshape(CHIPS, cols, width)

    acc[...] = jnp.zeros_like(acc)

    def backward(q, _):
        values = curv[q]
        shifted = []
        for tap in range(9):
            offset, valid = tap_of(tap)
            term = values * valid
            shifted.append(term if offset == 0 else pltpu.roll(term, offset % width, 1))
        features = hid[pl.ds(2 * q, 2)].reshape(width, channels)
        acc[...] += jnp.dot(
            jnp.concatenate(shifted, axis=0).astype(BF16), features, preferred_element_type=F32
        )
        return 0

    lax.fori_loop(0, CHIPS, backward, 0)
    flat = w_flat
    for tap in range(9):
        flat[:cols, tap * channels : (tap + 1) * channels] = acc[tap * cols : (tap + 1) * cols]
    r_rows = r_out.shape[1]
    for d in range(n):
        start, size = window_of(d * share, share, kernel_rows)
        piece = flat[: r_rows, start : start + size]
        if d * share > start:
            piece = pltpu.roll(piece, (start - d * share) % size, 1)
        r_out[d] = piece[:, :rows].astype(BF16)

    def send_sums(k, _):
        target = lax.rem(me + k, n)
        remote(r_out.at[target], r_buf.at[me], r_send, r_recv, target).start()
        return 0

    lax.fori_loop(1, n, send_sums, 0)
    r_own = pltpu.make_async_copy(r_out.at[me], r_buf.at[me], r_recv)
    r_own.start()
    remote(r_buf, r_buf, r_send, r_recv, partner).wait_recv()
    for b in range(BLOCK):
        total = r_buf[b].astype(F32)
        for other in range(b + BLOCK, n, BLOCK):
            total = total + r_buf[other].astype(F32)
        out[b * cols : (b + 1) * cols] = total[:cols]

    lat_copy.wait_send()
    tgt_copy.wait_send()
    others = pl.ds(0, n - 1)
    remote(w_buf.at[others], w_buf.at[others], w_send, w_recv, partner).wait_send()
    peers = pl.ds(0, BLOCK - 1)
    remote(hid.at[peers], hid.at[peers], h_send, h_recv, partner).wait_send()
    chips = pl.ds(0, CHIPS - 1)
    remote(t_buf.at[chips], t_buf.at[chips], t_send, t_recv, partner).wait_send()
    remote(r_buf.at[others], r_buf.at[others], r_send, r_recv, partner).wait_send()


def per_device(latents, targets, heights, widths, owner, weight, probe):
    n = lax.axis_size("dp")
    slots, frame_rows, frame_cols, channels = latents.shape
    cells = frame_rows * frame_cols
    share, out_channels = weight.shape
    owned = slots // 2
    pair = 2 * owned
    width = pair * cells
    cols = out_channels // BLOCK
    rows = up(share, LANES)
    kernel_rows = share * n
    me = lax.axis_index("dp")
    base = me // BLOCK * BLOCK

    def of_block(values):
        return lax.dynamic_slice_in_dim(values, base * slots, BLOCK * slots).reshape(
            CHIPS, 2 * slots
        )

    live = of_block(owner) >= 0
    index = jnp.arange(2 * slots, dtype=jnp.int32)
    before = index[None, :] < index[:, None]
    rank = jnp.sum((live[:, None, :] & before[None]).astype(jnp.int32), axis=2)
    taken = (
        (rank[:, None, :] == jnp.arange(pair, dtype=jnp.int32)[None, :, None]) & live[:, None, :]
    ).astype(jnp.int32)
    slot = jnp.sum(taken * index[None, None, :], axis=2)
    tall = jnp.sum(taken * of_block(heights)[:, None, :], axis=2)
    broad = jnp.sum(taken * of_block(widths)[:, None, :], axis=2)
    place = jnp.arange(cells, dtype=jnp.int32)
    mask = (
        (place[None, None, :] // frame_cols < tall[:, :, None])
        & (place[None, None, :] % frame_cols < broad[:, :, None])
    ).astype(F32)
    mask = jnp.broadcast_to(mask.reshape(CHIPS, 1, width), (CHIPS, 8, width))
    chip = (me - base) // 2

    def mine(values):
        return lax.dynamic_index_in_dim(values, chip, 0, keepdims=False)

    both = jnp.concatenate(
        [weight.T.reshape(BLOCK, cols, share), probe.T.reshape(BLOCK, cols, share)], axis=1
    )
    both = jnp.pad(both, ((0, 0), (0, 0), (0, rows - share)))
    padded = up(cols, 16)
    smem = pl.BlockSpec(memory_space=pltpu.SMEM)
    vmem = pl.BlockSpec(memory_space=pltpu.VMEM)
    sem = pltpu.SemaphoreType.DMA
    scratch = [
        pltpu.VMEM((2, slots, cells, channels), BF16),
        pltpu.VMEM((2, slots, cells, out_channels), BF16),
        pltpu.VMEM((n, 2 * cols, rows), BF16),
        pltpu.VMEM((2 * cols, kernel_rows), F32),
        pltpu.VMEM((9 * 2 * cols, channels), BF16),
        pltpu.VMEM((BLOCK, owned * cells, channels), BF16),
        pltpu.VMEM((BLOCK, padded, width), BF16),
        pltpu.VMEM((CHIPS, padded, width), BF16),
        pltpu.VMEM((9 * 2 * cols, width), F32),
        pltpu.VMEM((CHIPS, cols, width), F32),
        pltpu.VMEM((CHIPS, cols, width), F32),
        pltpu.VMEM((CHIPS, cols, width), F32),
        pltpu.VMEM((9 * cols, channels), F32),
        pltpu.VMEM((n, padded, rows), BF16),
        pltpu.VMEM((n, padded, rows), BF16),
    ] + [sem] * 12
    turned = pl.pallas_call(
        functools.partial(kernel, n, 1.0 / (owned * n)),
        out_shape=jax.ShapeDtypeStruct((out_channels, rows), F32),
        in_specs=[smem] * 3 + [vmem] * 4,
        out_specs=vmem,
        scratch_shapes=scratch,
        compiler_params=pltpu.CompilerParams(
            collective_id=0, has_side_effects=True, vmem_limit_bytes=56 * 2**20
        ),
    )(
        mine(slot),
        mine(tall),
        mine(broad),
        latents.reshape(slots, cells, channels),
        targets.reshape(slots, cells, out_channels),
        both,
        mask,
    )
    return turned[:, :share].T


def solution(mesh):
    return jax.shard_map(
        per_device,
        mesh=mesh,
        in_specs=(
            P(("groups", "dp"), None, None, None),
            P(("groups", "dp"), None, None, None),
            P("groups"),
            P("groups"),
            P("groups"),
            P("dp", None),
            P(("groups", "dp"), None),
        ),
        out_specs=P(("groups", "dp"), None),
        check_vma=False,
    )
```

```python
import functools

import jax
import jax.numpy as jnp
from jax import lax
from jax.experimental import pallas as pl
from jax.experimental.pallas import tpu as pltpu
from jax.sharding import PartitionSpec as P

PER_GROUP = 20
EPSILON = 1e-05
BLOCK = 8
CHIPS = BLOCK // 2
CELLS = 64
LANES = 128
MESH = pl.DeviceIdType.MESH
F32 = jnp.float32
BF16 = jnp.bfloat16


def up(value, step):
    return -(-value // step) * step


def thirds(value):
    high = value.astype(BF16)
    rest = value - high.astype(F32)
    mid = rest.astype(BF16)
    low = (rest - mid.astype(F32)).astype(BF16)
    return high, mid, low


def times_onehot(value, onehot):
    rows = value.shape[0]
    stacked = jnp.concatenate(
        [part.astype(F32) for part in thirds(value)], axis=0
    ).astype(BF16)
    product = jnp.dot(stacked, onehot, preferred_element_type=F32)
    return product[:rows] + product[rows : 2 * rows] + product[2 * rows :]


def onehot_times(onehot, value):
    high, mid, low = thirds(value)
    dot = functools.partial(jnp.dot, preferred_element_type=F32)
    return dot(onehot, high) + dot(onehot, mid) + dot(onehot, low)


def between(inner, outer, width):
    return (inner >= outer * width) & (inner < outer * width + width)


def iota(shape, axis):
    return lax.broadcasted_iota(jnp.int32, shape, axis)


def window_of(start, width, total):
    size = min(up(width + LANES - 1, LANES), total)
    return min(start // LANES * LANES, total - size), size


def kernel(
    n, factor, pick, high, wide, lat_in, tgt_in, w_in, mask_in, out,
    lat, tgt, w_buf, w_flat, wall, hid, t_out, t_buf, z, u_buf, t_tan, curv, acc, r_out, r_buf,
    lat_send, lat_recv, tgt_send, tgt_recv, w_send, w_recv, h_send, h_recv, t_send, t_recv,
    r_send, r_recv,
):
    me = lax.axis_index("dp")
    pos = lax.rem(me, BLOCK)
    base = me - pos
    chip = pos // 2
    core = lax.rem(pos, 2)
    partner = me + 1 - 2 * core
    slots = lat_in.shape[0]
    owned = slots // 2
    pair = 2 * owned
    width = pair * CELLS
    half = owned * CELLS
    channels = lat_in.shape[2]
    rows = w_rows = out.shape[1]
    del w_rows
    cols = out.shape[0] // BLOCK
    kernel_rows = w_flat.shape[1]
    share = kernel_rows // n

    barrier = pltpu.get_barrier_semaphore()

    def greet(k, _):
        pl.semaphore_signal(
            barrier, inc=1, device_id={"dp": lax.rem(me + k, n)}, device_id_type=MESH
        )
        return 0

    lax.fori_loop(1, n, greet, 0)
    pl.semaphore_wait(barrier, n - 1)

    def remote(src, dst, send, recv, target):
        return pltpu.make_async_remote_copy(
            src_ref=src, dst_ref=dst, send_sem=send, recv_sem=recv,
            device_id={"dp": target}, device_id_type=MESH,
        )

    lat_copy = remote(lat_in, lat.at[core], lat_send, lat_recv, partner)
    lat_copy.start()
    tgt_copy = remote(tgt_in, tgt.at[core], tgt_send, tgt_recv, partner)
    tgt_copy.start()

    def send_w(k, _):
        target = lax.rem(me + k, n)
        remote(w_in.at[lax.rem(target, BLOCK)], w_buf.at[me], w_send, w_recv, target).start()
        return 0

    lax.fori_loop(1, n, send_w, 0)
    w_own = pltpu.make_async_copy(w_in.at[pos], w_buf.at[me], w_recv)
    w_own.start()
    lat[core] = lat_in[...]
    tgt[core] = tgt_in[...]
    lat_copy.wait_recv()

    to_group = between(
        iota((channels, LANES), 0), iota((channels, LANES), 1), PER_GROUP
    ).astype(F32).astype(BF16)
    from_group = between(
        iota((LANES, channels), 1), iota((LANES, channels), 0), PER_GROUP
    ).astype(F32).astype(BF16)
    cell = iota((CELLS, channels), 0)
    cell_row, cell_col = cell >> 3, cell & 7
    frames, inside, counts = [], [], []
    for k in range(owned):
        which = pick[core * owned + k]
        tall, broad = high[core * owned + k], wide[core * owned + k]
        frames.append(lat[which // slots, lax.rem(which, slots)].astype(F32))
        inside.append(((cell_row < tall) & (cell_col < broad)).astype(F32))
        counts.append(jnp.full((1, LANES), tall * broad * PER_GROUP, jnp.int32).astype(F32))
    spare = 8 - owned
    counts = jnp.concatenate(counts + [jnp.ones((spare, LANES), F32)], axis=0)

    def group_mean(values):
        sums = [jnp.sum(v * m, axis=0, keepdims=True) for v, m in zip(values, inside)]
        sums = jnp.concatenate(sums + [jnp.zeros((spare, channels), F32)], axis=0)
        return times_onehot(sums, to_group) / counts

    mean = times_onehot(group_mean(frames), from_group)
    centred = [v - mean[k : k + 1] for k, v in enumerate(frames)]
    square = group_mean([v * v for v in centred])
    scale = times_onehot(lax.rsqrt(square + EPSILON), from_group)
    for k in range(owned):
        x = centred[k] * scale[k : k + 1]
        hid[pos, k * CELLS : (k + 1) * CELLS] = (
            x / (1.0 + jnp.exp(-x)) * inside[k]
        ).astype(BF16)

    side = chip + 1 - 2 * lax.rem(chip, 2)
    ahead = lax.rem(chip + 2, CHIPS)
    across = lax.rem(side + 2, CHIPS)
    chips = (chip, side, ahead, across)

    def pass_on(which, position, piece, target):
        part = hid.at[position] if piece is None else hid.at[position, pl.ds(piece * quarter, quarter)]
        copy = remote(part, part, h_send.at[which], h_recv.at[which], target)
        copy.start()
        return copy

    quarter = half // 2
    passed = [
        pass_on(1, pos, None, base + 2 * side + core),
        pass_on(2, pos, None, base + 2 * ahead + core),
        pass_on(0, pos, None, partner),
    ]

    def arrived(which, piece):
        part = hid.at[pos] if piece is None else hid.at[pos, pl.ds(piece * quarter, quarter)]
        remote(part, part, h_send.at[which], h_recv.at[which], partner).wait_recv()

    tgt_copy.wait_recv()
    chosen = []
    for k in range(pair):
        which = pick[k]
        chosen.append(tgt[which // slots, lax.rem(which, slots)].astype(F32))
    turned = jnp.concatenate(chosen, axis=0).T
    t_rows = t_out.shape[1]
    for b in range(BLOCK):
        t_out[b] = jnp.concatenate(
            [turned[b * cols : (b + 1) * cols], jnp.zeros((t_rows - cols, width), F32)], axis=0
        ).astype(BF16)
    t_buf[chip] = t_out[pos]

    def send_targets(k, _):
        there = 2 * lax.rem(chip + k, CHIPS) + core
        remote(t_out.at[there], t_buf.at[chip], t_send, t_recv, base + there).start()
        return 0

    lax.fori_loop(1, CHIPS, send_targets, 0)

    arrived(1, None)
    passed.append(pass_on(3, 2 * side + core, 0, base + 2 * ahead + core))
    passed.append(pass_on(5, 2 * side + core, None, partner))
    arrived(2, None)
    passed.append(pass_on(4, 2 * ahead + core, 1, base + 2 * side + core))
    passed.append(pass_on(6, 2 * ahead + core, None, partner))

    remote(w_buf, w_buf, w_send, w_recv, partner).wait_recv()
    w_flat[...] = jnp.zeros_like(w_flat)
    for d in range(n):
        start, size = window_of(d * share, share, kernel_rows)
        piece = w_buf[d].astype(F32)
        lane = iota(piece.shape, 1)
        piece = jnp.where(lane < share, piece, 0.0)
        if size > rows:
            piece = jnp.concatenate(
                [piece, jnp.zeros((piece.shape[0], size - rows), F32)], axis=1
            )
        if d * share > start:
            piece = pltpu.roll(piece, d * share - start, 1)
        w_flat[:, start : start + size] += piece
    both = 2 * cols
    for tap in range(9):
        wall[tap * both : (tap + 1) * both] = w_flat[
            :, tap * channels : (tap + 1) * channels
        ].astype(BF16)

    lane = iota((1, width), 1)
    lane_row, lane_col = (lane >> 3) & 7, lane & 7

    def tap_of(tap):
        a, b = tap // 3 - 1, tap % 3 - 1
        valid = (
            (lane_row + a >= 0) & (lane_row + a < 8) & (lane_col + b >= 0) & (lane_col + b < 8)
        )
        return a * 8 + b, valid.astype(F32)

    def forward(q, place):
        features = hid[pl.ds(2 * q, 2)].reshape(width, channels)
        z[...] = lax.dot_general(
            wall[...], features, (((1,), (1,)), ((), ())), preferred_element_type=F32
        )
        total = z[4 * both : 5 * both]
        for tap in range(9):
            if tap != 4:
                offset, valid = tap_of(tap)
                total = total + valid * pltpu.roll(
                    z[tap * both : (tap + 1) * both], -offset % width, 1
                )
        u_buf[place * cols : (place + 1) * cols] = total[:cols]
        t_tan[place * cols : (place + 1) * cols] = total[cols:]

    wide_rows = 2 * cols
    to_sample = between(
        iota((width, LANES), 0), iota((width, LANES), 1), CELLS
    ).astype(F32).astype(BF16)
    from_sample = between(
        iota((LANES, width), 1), iota((LANES, width), 0), CELLS
    ).astype(F32).astype(BF16)
    row, col = iota((wide_rows, LANES), 0), iota((wide_rows, LANES), 1)
    to_norm = between(row, col, PER_GROUP).astype(F32).astype(BF16)
    row, col = iota((LANES, wide_rows), 1), iota((LANES, wide_rows), 0)
    of_norm = between(row, col, PER_GROUP).astype(F32).astype(BF16)

    def second_order(near, far):
        mask = jnp.concatenate(
            [jnp.broadcast_to(mask_in[q, 0:1], (cols, width)) for q in (near, far)], axis=0
        )
        per_sample = jnp.dot(mask.astype(BF16), to_sample, preferred_element_type=F32)
        inverse = 1.0 / (jnp.maximum(per_sample, 1.0) * PER_GROUP)

        def small(*values):
            sums = times_onehot(jnp.concatenate(values, axis=0), to_sample)
            sums = jnp.concatenate(
                [sums[k * wide_rows : (k + 1) * wide_rows] for k in range(len(values))], axis=1
            )
            sums = onehot_times(to_norm, onehot_times(of_norm, sums))
            return [
                sums[:, k * LANES : (k + 1) * LANES] * inverse for k in range(len(values))
            ]

        def spread(*values):
            back = times_onehot(jnp.concatenate(values, axis=0), from_sample)
            return [back[k * wide_rows : (k + 1) * wide_rows] for k in range(len(values))]

        u = u_buf[...]
        t = t_tan[...]
        u_mean, t_mean = spread(*small(u * mask, t * mask))
        c = u - u_mean
        (square,) = small(c * c * mask)
        (r,) = spread(lax.rsqrt(square + EPSILON))
        x = c * r
        wanted = jnp.concatenate([t_buf[q].astype(F32)[:cols] for q in (near, far)], axis=0)
        sigma = 1.0 / (1.0 + jnp.exp(-x))
        missing = x * sigma - wanted
        first = sigma * (1.0 + x * (1.0 - sigma))
        second = sigma * (1.0 - sigma) * (2.0 + x * (1.0 - 2.0 * sigma))
        weight = factor * mask
        g = weight * missing * first
        a, g_mean, b = spread(*small(x * t * mask, g, g * x))
        x_dot = r * (t - t_mean - x * a)
        g_dot = weight * (first * first + missing * second) * x_dot
        h = g - g_mean - x * b
        g_dot_mean, b_dot = spread(*small(g_dot, g_dot * x + g * x_dot))
        h_dot = g_dot - g_dot_mean - x_dot * b - x * b_dot
        curv[...] = mask * (r * h_dot - r * r * a * h)

    def backward(q, place, adds):
        values = curv[place * cols : (place + 1) * cols]
        shifted = []
        for tap in range(9):
            offset, valid = tap_of(tap)
            term = values * valid
            shifted.append(term if offset == 0 else pltpu.roll(term, offset % width, 1))
        features = hid[pl.ds(2 * q, 2)].reshape(width, channels)
        product = jnp.dot(
            jnp.concatenate(shifted, axis=0).astype(BF16), features, preferred_element_type=F32
        )
        acc[...] = acc[...] + product if adds else product

    arrived(0, None)
    forward(chip, 0)
    arrived(5, None)
    forward(side, 1)
    remote(
        t_buf.at[pl.ds(0, CHIPS - 1)], t_buf.at[pl.ds(0, CHIPS - 1)], t_send, t_recv, partner
    ).wait_recv()
    second_order(chip, side)
    arrived(3, 0)
    passed.append(pass_on(7, 2 * across + core, 0, partner))
    arrived(4, 1)
    passed.append(pass_on(8, 2 * across + core, 1, partner))
    backward(chip, 0, False)
    backward(side, 1, True)
    arrived(6, None)
    forward(ahead, 0)
    arrived(7, 0)
    arrived(8, 1)
    forward(across, 1)
    second_order(ahead, across)
    backward(ahead, 0, True)
    backward(across, 1, True)
    flat = w_flat
    for tap in range(9):
        flat[:cols, tap * channels : (tap + 1) * channels] = acc[tap * cols : (tap + 1) * cols]
    tiles = rows // LANES
    r_rows = r_out.shape[1]
    for d in range(n):
        start, size = window_of(d * share, share, kernel_rows)
        piece = flat[:cols, start : start + size]
        if d * share > start:
            piece = pltpu.roll(piece, (start - d * share) % size, 1)
        stacked = [piece[:, k * LANES : (k + 1) * LANES] for k in range(tiles)]
        if r_rows > tiles * cols:
            stacked.append(jnp.zeros((r_rows - tiles * cols, LANES), F32))
        r_out[d] = jnp.concatenate(stacked, axis=0).astype(BF16)

    def send_sums(k, _):
        target = lax.rem(me + k, n)
        remote(r_out.at[target], r_buf.at[me], r_send, r_recv, target).start()
        return 0

    lax.fori_loop(1, n, send_sums, 0)
    r_own = pltpu.make_async_copy(r_out.at[me], r_buf.at[me], r_recv)
    r_own.start()
    remote(r_buf, r_buf, r_send, r_recv, partner).wait_recv()
    for b in range(BLOCK):
        total = r_buf[b].astype(F32)
        for other in range(b + BLOCK, n, BLOCK):
            total = total + r_buf[other].astype(F32)
        for k in range(tiles):
            out[b * cols : (b + 1) * cols, k * LANES : (k + 1) * LANES] = total[
                k * cols : (k + 1) * cols
            ]

    lat_copy.wait_send()
    tgt_copy.wait_send()
    others = pl.ds(0, n - 1)
    remote(w_buf.at[others], w_buf.at[others], w_send, w_recv, partner).wait_send()
    for copy in passed:
        copy.wait_send()
    three = pl.ds(0, CHIPS - 1)
    remote(t_buf.at[three], t_buf.at[three], t_send, t_recv, partner).wait_send()
    remote(r_buf.at[others], r_buf.at[others], r_send, r_recv, partner).wait_send()


def per_device(latents, targets, heights, widths, owner, weight, probe):
    n = lax.axis_size("dp")
    slots, frame_rows, frame_cols, channels = latents.shape
    cells = frame_rows * frame_cols
    share, out_channels = weight.shape
    owned = slots // 2
    pair = 2 * owned
    width = pair * cells
    cols = out_channels // BLOCK
    rows = up(share, LANES)
    kernel_rows = share * n
    me = lax.axis_index("dp")
    base = me // BLOCK * BLOCK

    def of_block(values):
        return lax.dynamic_slice_in_dim(values, base * slots, BLOCK * slots).reshape(
            CHIPS, 2 * slots
        )

    live = of_block(owner) >= 0
    index = jnp.arange(2 * slots, dtype=jnp.int32)
    before = index[None, :] < index[:, None]
    rank = jnp.sum((live[:, None, :] & before[None]).astype(jnp.int32), axis=2)
    taken = (
        (rank[:, None, :] == jnp.arange(pair, dtype=jnp.int32)[None, :, None]) & live[:, None, :]
    ).astype(jnp.int32)
    slot = jnp.sum(taken * index[None, None, :], axis=2)
    tall = jnp.sum(taken * of_block(heights)[:, None, :], axis=2)
    broad = jnp.sum(taken * of_block(widths)[:, None, :], axis=2)
    place = jnp.arange(cells, dtype=jnp.int32)
    mask = (
        (place[None, None, :] // frame_cols < tall[:, :, None])
        & (place[None, None, :] % frame_cols < broad[:, :, None])
    ).astype(F32)
    mask = jnp.broadcast_to(mask.reshape(CHIPS, 1, width), (CHIPS, 8, width))
    chip = (me - base) // 2

    def mine(values):
        return lax.dynamic_index_in_dim(values, chip, 0, keepdims=False)

    both = jnp.concatenate(
        [weight.T.reshape(BLOCK, cols, share), probe.T.reshape(BLOCK, cols, share)], axis=1
    )
    both = jnp.pad(both, ((0, 0), (0, 0), (0, rows - share)))
    padded = up(cols, 16)
    smem = pl.BlockSpec(memory_space=pltpu.SMEM)
    vmem = pl.BlockSpec(memory_space=pltpu.VMEM)
    sem = pltpu.SemaphoreType.DMA
    scratch = [
        pltpu.VMEM((2, slots, cells, channels), BF16),
        pltpu.VMEM((2, slots, cells, out_channels), BF16),
        pltpu.VMEM((n, 2 * cols, rows), BF16),
        pltpu.VMEM((2 * cols, kernel_rows), F32),
        pltpu.VMEM((9 * 2 * cols, channels), BF16),
        pltpu.VMEM((BLOCK, owned * cells, channels), BF16),
        pltpu.VMEM((BLOCK, padded, width), BF16),
        pltpu.VMEM((CHIPS, padded, width), BF16),
        pltpu.VMEM((9 * 2 * cols, width), F32),
        pltpu.VMEM((2 * cols, width), F32),
        pltpu.VMEM((2 * cols, width), F32),
        pltpu.VMEM((2 * cols, width), F32),
        pltpu.VMEM((9 * cols, channels), F32),
        pltpu.VMEM((n, up(cols * rows // LANES, 16), LANES), BF16),
        pltpu.VMEM((n, up(cols * rows // LANES, 16), LANES), BF16),
    ] + [sem] * 6 + [sem((9,))] * 2 + [sem] * 4
    turned = pl.pallas_call(
        functools.partial(kernel, n, 1.0 / (owned * n)),
        out_shape=jax.ShapeDtypeStruct((out_channels, rows), F32),
        in_specs=[smem] * 3 + [vmem] * 4,
        out_specs=vmem,
        scratch_shapes=scratch,
        compiler_params=pltpu.CompilerParams(
            collective_id=0, has_side_effects=True, vmem_limit_bytes=56 * 2**20
        ),
    )(
        mine(slot),
        mine(tall),
        mine(broad),
        latents.reshape(slots, cells, channels),
        targets.reshape(slots, cells, out_channels),
        both,
        mask,
    )
    return turned[:, :share].T


def solution(mesh):
    return jax.shard_map(
        per_device,
        mesh=mesh,
        in_specs=(
            P(("groups", "dp"), None, None, None),
            P(("groups", "dp"), None, None, None),
            P("groups"),
            P("groups"),
            P("groups"),
            P("dp", None),
            P(("groups", "dp"), None),
        ),
        out_specs=P(("groups", "dp"), None),
        check_vma=False,
    )
```

```python
import functools

import jax
import jax.numpy as jnp
from jax import lax
from jax.experimental import pallas as pl
from jax.experimental.pallas import tpu as pltpu
from jax.sharding import PartitionSpec as P

PER_GROUP = 20
EPSILON = 1e-05
BLOCK = 8
CHIPS = BLOCK // 2
CELLS = 64
LANES = 128
MESH = pl.DeviceIdType.MESH
F32 = jnp.float32
BF16 = jnp.bfloat16


def up(value, step):
    return -(-value // step) * step


def thirds(value):
    high = value.astype(BF16)
    rest = value - high.astype(F32)
    mid = rest.astype(BF16)
    low = (rest - mid.astype(F32)).astype(BF16)
    return high, mid, low


def times_onehot(value, onehot):
    rows = value.shape[0]
    stacked = jnp.concatenate(
        [part.astype(F32) for part in thirds(value)], axis=0
    ).astype(BF16)
    product = jnp.dot(stacked, onehot, preferred_element_type=F32)
    return product[:rows] + product[rows : 2 * rows] + product[2 * rows :]


def onehot_times(onehot, value):
    high, mid, low = thirds(value)
    dot = functools.partial(jnp.dot, preferred_element_type=F32)
    return dot(onehot, high) + dot(onehot, mid) + dot(onehot, low)


def between(inner, outer, width):
    return (inner >= outer * width) & (inner < outer * width + width)


def iota(shape, axis):
    return lax.broadcasted_iota(jnp.int32, shape, axis)


def window_of(start, width, total):
    size = min(up(width + LANES - 1, LANES), total)
    return min(start // LANES * LANES, total - size), size


def kernel(
    n, factor, table, lat_in, tgt_in, w_in, mask_in, out,
    lat, tgt, w_buf, w_flat, wall, hid, t_out, t_buf, z, u_buf, t_tan, curv, acc, r_out, r_buf,
    lat_send, lat_recv, tgt_send, tgt_recv, w_send, w_recv, h_send, h_recv, t_send, t_recv,
    r_send, r_recv,
):
    me = lax.axis_index("dp")
    pos = lax.rem(me, BLOCK)
    base = me - pos
    chip = pos // 2
    core = lax.rem(pos, 2)
    partner = me + 1 - 2 * core
    slots = lat_in.shape[0]
    owned = slots // 2
    pair = 2 * owned
    width = pair * CELLS
    half = owned * CELLS
    channels = lat_in.shape[2]
    rows = w_rows = out.shape[1]
    del w_rows
    cols = out.shape[0] // BLOCK
    kernel_rows = w_flat.shape[1]
    share = kernel_rows // n

    barrier = pltpu.get_barrier_semaphore()

    def greet(k, _):
        pl.semaphore_signal(
            barrier, inc=1, device_id={"dp": lax.rem(me + k, n)}, device_id_type=MESH
        )
        return 0

    lax.fori_loop(1, n, greet, 0)
    pl.semaphore_wait(barrier, n - 1)

    def remote(src, dst, send, recv, target):
        return pltpu.make_async_remote_copy(
            src_ref=src, dst_ref=dst, send_sem=send, recv_sem=recv,
            device_id={"dp": target}, device_id_type=MESH,
        )

    lat_copy = remote(lat_in, lat.at[core], lat_send, lat_recv, partner)
    lat_copy.start()
    tgt_copy = remote(tgt_in, tgt.at[core], tgt_send, tgt_recv, partner)
    tgt_copy.start()

    def send_w(k, _):
        target = lax.rem(me + k, n)
        remote(w_in.at[lax.rem(target, BLOCK)], w_buf.at[me], w_send, w_recv, target).start()
        return 0

    lax.fori_loop(1, n, send_w, 0)
    w_own = pltpu.make_async_copy(w_in.at[pos], w_buf.at[me], w_recv)
    w_own.start()
    lat[core] = lat_in[...]
    tgt[core] = tgt_in[...]
    lat_copy.wait_recv()

    to_group = between(
        iota((channels, LANES), 0), iota((channels, LANES), 1), PER_GROUP
    ).astype(F32).astype(BF16)
    from_group = between(
        iota((LANES, channels), 1), iota((LANES, channels), 0), PER_GROUP
    ).astype(F32).astype(BF16)
    cell = iota((CELLS, channels), 0)
    cell_row, cell_col = cell >> 3, cell & 7
    frames, inside, counts = [], [], []
    for k in range(owned):
        which, tall, broad = (
            table[(CHIPS * field + chip) * pair + core * owned + k] for field in range(3)
        )
        frames.append(lat[which // slots, lax.rem(which, slots)].astype(F32))
        inside.append(((cell_row < tall) & (cell_col < broad)).astype(F32))
        counts.append(jnp.full((1, LANES), tall * broad * PER_GROUP, jnp.int32).astype(F32))
    spare = 8 - owned
    counts = jnp.concatenate(counts + [jnp.ones((spare, LANES), F32)], axis=0)

    def group_mean(values):
        sums = [jnp.sum(v * m, axis=0, keepdims=True) for v, m in zip(values, inside)]
        sums = jnp.concatenate(sums + [jnp.zeros((spare, channels), F32)], axis=0)
        return times_onehot(sums, to_group) / counts

    mean = times_onehot(group_mean(frames), from_group)
    centred = [v - mean[k : k + 1] for k, v in enumerate(frames)]
    square = group_mean([v * v for v in centred])
    scale = times_onehot(lax.rsqrt(square + EPSILON), from_group)
    for k in range(owned):
        x = centred[k] * scale[k : k + 1]
        hid[pos, k * CELLS : (k + 1) * CELLS] = (
            x / (1.0 + jnp.exp(-x)) * inside[k]
        ).astype(BF16)

    side = chip + 1 - 2 * lax.rem(chip, 2)
    ahead = lax.rem(chip + 2, CHIPS)
    across = lax.rem(side + 2, CHIPS)
    chips = (chip, side, ahead, across)

    def pass_on(which, position, piece, target):
        part = hid.at[position] if piece is None else hid.at[position, pieces[piece]]
        copy = remote(part, part, h_send.at[which], h_recv.at[which], target)
        copy.start()
        return copy

    small_part = half // 4
    pieces = (pl.ds(0, small_part), pl.ds(small_part, half - small_part))
    passed = [
        pass_on(1, pos, None, base + 2 * side + core),
        pass_on(2, pos, None, base + 2 * ahead + core),
        pass_on(0, pos, None, partner),
    ]

    def arrived(which, piece):
        part = hid.at[pos] if piece is None else hid.at[pos, pieces[piece]]
        remote(part, part, h_send.at[which], h_recv.at[which], partner).wait_recv()

    tgt_copy.wait_recv()
    chosen = []
    for k in range(pair):
        which = table[chip * pair + k]
        chosen.append(tgt[which // slots, lax.rem(which, slots)].astype(F32))
    turned = jnp.concatenate(chosen, axis=0).T
    t_rows = t_out.shape[1]
    for b in range(BLOCK):
        t_out[b] = jnp.concatenate(
            [turned[b * cols : (b + 1) * cols], jnp.zeros((t_rows - cols, width), F32)], axis=0
        ).astype(BF16)
    t_buf[chip] = t_out[pos]

    def send_targets(k, _):
        there = 2 * lax.rem(chip + k, CHIPS) + core
        remote(t_out.at[there], t_buf.at[chip], t_send, t_recv, base + there).start()
        return 0

    lax.fori_loop(1, CHIPS, send_targets, 0)

    arrived(1, None)
    passed.append(pass_on(3, 2 * side + core, 0, base + 2 * ahead + core))
    passed.append(pass_on(5, 2 * side + core, None, partner))
    arrived(2, None)
    passed.append(pass_on(4, 2 * ahead + core, 1, base + 2 * side + core))
    passed.append(pass_on(6, 2 * ahead + core, None, partner))

    remote(w_buf, w_buf, w_send, w_recv, partner).wait_recv()
    w_flat[...] = jnp.zeros_like(w_flat)
    for d in range(n):
        start, size = window_of(d * share, share, kernel_rows)
        piece = w_buf[d].astype(F32)
        lane = iota(piece.shape, 1)
        piece = jnp.where(lane < share, piece, 0.0)
        if size > rows:
            piece = jnp.concatenate(
                [piece, jnp.zeros((piece.shape[0], size - rows), F32)], axis=1
            )
        if d * share > start:
            piece = pltpu.roll(piece, d * share - start, 1)
        w_flat[:, start : start + size] += piece
    both = 2 * cols
    for tap in range(9):
        wall[tap * both : (tap + 1) * both] = w_flat[
            :, tap * channels : (tap + 1) * channels
        ].astype(BF16)

    lane = iota((1, width), 1)
    lane_row, lane_col = (lane >> 3) & 7, lane & 7

    def tap_of(tap):
        a, b = tap // 3 - 1, tap % 3 - 1
        valid = (
            (lane_row + a >= 0) & (lane_row + a < 8) & (lane_col + b >= 0) & (lane_col + b < 8)
        )
        return a * 8 + b, valid.astype(F32)

    def forward(q, place):
        features = hid[pl.ds(2 * q, 2)].reshape(width, channels)
        z[...] = lax.dot_general(
            wall[...], features, (((1,), (1,)), ((), ())), preferred_element_type=F32
        )
        total = z[4 * both : 5 * both]
        for tap in range(9):
            if tap != 4:
                offset, valid = tap_of(tap)
                total = total + valid * pltpu.roll(
                    z[tap * both : (tap + 1) * both], -offset % width, 1
                )
        u_buf[place * cols : (place + 1) * cols] = total[:cols]
        t_tan[place * cols : (place + 1) * cols] = total[cols:]

    to_sample = between(
        iota((width, LANES), 0), iota((width, LANES), 1), CELLS
    ).astype(F32).astype(BF16)
    from_sample = between(
        iota((LANES, width), 1), iota((LANES, width), 0), CELLS
    ).astype(F32).astype(BF16)

    def second_order(*those):
        wide_rows = len(those) * cols
        row, col = iota((wide_rows, LANES), 0), iota((wide_rows, LANES), 1)
        to_norm = between(row, col, PER_GROUP).astype(F32).astype(BF16)
        row, col = iota((LANES, wide_rows), 1), iota((LANES, wide_rows), 0)
        of_norm = between(row, col, PER_GROUP).astype(F32).astype(BF16)
        mask = jnp.concatenate(
            [jnp.broadcast_to(mask_in[q, 0:1], (cols, width)) for q in those], axis=0
        )
        per_sample = jnp.dot(mask.astype(BF16), to_sample, preferred_element_type=F32)
        inverse = 1.0 / (jnp.maximum(per_sample, 1.0) * PER_GROUP)

        def small(*values):
            sums = times_onehot(jnp.concatenate(values, axis=0), to_sample)
            sums = jnp.concatenate(
                [sums[k * wide_rows : (k + 1) * wide_rows] for k in range(len(values))], axis=1
            )
            sums = onehot_times(to_norm, onehot_times(of_norm, sums))
            return [
                sums[:, k * LANES : (k + 1) * LANES] * inverse for k in range(len(values))
            ]

        def spread(*values):
            back = times_onehot(jnp.concatenate(values, axis=0), from_sample)
            return [back[k * wide_rows : (k + 1) * wide_rows] for k in range(len(values))]

        u = u_buf[:wide_rows]
        t = t_tan[:wide_rows]
        u_mean, t_mean = spread(*small(u * mask, t * mask))
        c = u - u_mean
        (square,) = small(c * c * mask)
        (r,) = spread(lax.rsqrt(square + EPSILON))
        x = c * r
        wanted = jnp.concatenate([t_buf[q].astype(F32)[:cols] for q in those], axis=0)
        sigma = 1.0 / (1.0 + jnp.exp(-x))
        missing = x * sigma - wanted
        first = sigma * (1.0 + x * (1.0 - sigma))
        second = sigma * (1.0 - sigma) * (2.0 + x * (1.0 - 2.0 * sigma))
        weight = factor * mask
        g = weight * missing * first
        a, g_mean, b = spread(*small(x * t * mask, g, g * x))
        x_dot = r * (t - t_mean - x * a)
        g_dot = weight * (first * first + missing * second) * x_dot
        h = g - g_mean - x * b
        g_dot_mean, b_dot = spread(*small(g_dot, g_dot * x + g * x_dot))
        h_dot = g_dot - g_dot_mean - x_dot * b - x * b_dot
        curv[:wide_rows] = mask * (r * h_dot - r * r * a * h)

    def backward(q, place, adds):
        values = curv[place * cols : (place + 1) * cols]
        shifted = []
        for tap in range(9):
            offset, valid = tap_of(tap)
            term = values * valid
            shifted.append(term if offset == 0 else pltpu.roll(term, offset % width, 1))
        features = hid[pl.ds(2 * q, 2)].reshape(width, channels)
        product = jnp.dot(
            jnp.concatenate(shifted, axis=0).astype(BF16), features, preferred_element_type=F32
        )
        acc[...] = acc[...] + product if adds else product

    arrived(0, None)
    forward(chip, 0)
    arrived(5, None)
    forward(side, 1)
    remote(
        t_buf.at[pl.ds(0, CHIPS - 1)], t_buf.at[pl.ds(0, CHIPS - 1)], t_send, t_recv, partner
    ).wait_recv()
    arrived(6, None)
    forward(ahead, 2)
    second_order(chip, side, ahead)
    arrived(3, 0)
    passed.append(pass_on(7, 2 * across + core, 0, partner))
    arrived(4, 1)
    passed.append(pass_on(8, 2 * across + core, 1, partner))
    backward(chip, 0, False)
    backward(side, 1, True)
    backward(ahead, 2, True)
    arrived(7, 0)
    arrived(8, 1)
    forward(across, 0)
    second_order(across)
    backward(across, 0, True)
    flat = w_flat
    for tap in range(9):
        flat[:cols, tap * channels : (tap + 1) * channels] = acc[tap * cols : (tap + 1) * cols]
    tiles = rows // LANES
    r_rows = r_out.shape[1]
    for d in range(n):
        start, size = window_of(d * share, share, kernel_rows)
        piece = flat[:cols, start : start + size]
        if d * share > start:
            piece = pltpu.roll(piece, (start - d * share) % size, 1)
        stacked = [piece[:, k * LANES : (k + 1) * LANES] for k in range(tiles)]
        if r_rows > tiles * cols:
            stacked.append(jnp.zeros((r_rows - tiles * cols, LANES), F32))
        r_out[d] = jnp.concatenate(stacked, axis=0).astype(BF16)

    def send_sums(k, _):
        target = lax.rem(me + k, n)
        remote(r_out.at[target], r_buf.at[me], r_send, r_recv, target).start()
        return 0

    lax.fori_loop(1, n, send_sums, 0)
    r_own = pltpu.make_async_copy(r_out.at[me], r_buf.at[me], r_recv)
    r_own.start()
    remote(r_buf, r_buf, r_send, r_recv, partner).wait_recv()
    for b in range(BLOCK):
        total = r_buf[b].astype(F32)
        for other in range(b + BLOCK, n, BLOCK):
            total = total + r_buf[other].astype(F32)
        for k in range(tiles):
            out[b * cols : (b + 1) * cols, k * LANES : (k + 1) * LANES] = total[
                k * cols : (k + 1) * cols
            ]

    lat_copy.wait_send()
    tgt_copy.wait_send()
    others = pl.ds(0, n - 1)
    remote(w_buf.at[others], w_buf.at[others], w_send, w_recv, partner).wait_send()
    for copy in passed:
        copy.wait_send()
    three = pl.ds(0, CHIPS - 1)
    remote(t_buf.at[three], t_buf.at[three], t_send, t_recv, partner).wait_send()
    remote(r_buf.at[others], r_buf.at[others], r_send, r_recv, partner).wait_send()


def per_device(latents, targets, heights, widths, owner, weight, probe):
    n = lax.axis_size("dp")
    slots, frame_rows, frame_cols, channels = latents.shape
    cells = frame_rows * frame_cols
    share, out_channels = weight.shape
    owned = slots // 2
    pair = 2 * owned
    width = pair * cells
    cols = out_channels // BLOCK
    rows = up(share, LANES)
    kernel_rows = share * n
    me = lax.axis_index("dp")
    base = me // BLOCK * BLOCK

    def of_block(values):
        return lax.dynamic_slice_in_dim(values, base * slots, BLOCK * slots).reshape(
            CHIPS, 2 * slots
        )

    live = of_block(owner) >= 0
    index = jnp.arange(2 * slots, dtype=jnp.int32)
    before = index[None, :] < index[:, None]
    rank = jnp.sum((live[:, None, :] & before[None]).astype(jnp.int32), axis=2)
    taken = (
        (rank[:, None, :] == jnp.arange(pair, dtype=jnp.int32)[None, :, None]) & live[:, None, :]
    ).astype(jnp.int32)
    fields = jnp.stack(
        [jnp.broadcast_to(index, (CHIPS, 2 * slots)), of_block(heights), of_block(widths)]
    )
    table = jnp.sum(taken[None] * fields[:, :, None, :], axis=3)
    tall, broad = table[1], table[2]
    place = jnp.arange(cells, dtype=jnp.int32)
    mask = (
        (place[None, None, :] // frame_cols < tall[:, :, None])
        & (place[None, None, :] % frame_cols < broad[:, :, None])
    ).astype(F32)
    mask = jnp.broadcast_to(mask.reshape(CHIPS, 1, width), (CHIPS, 8, width))

    both = jnp.concatenate(
        [weight.T.reshape(BLOCK, cols, share), probe.T.reshape(BLOCK, cols, share)], axis=1
    )
    both = jnp.pad(both, ((0, 0), (0, 0), (0, rows - share)))
    padded = up(cols, 16)
    smem = pl.BlockSpec(memory_space=pltpu.SMEM)
    vmem = pl.BlockSpec(memory_space=pltpu.VMEM)
    sem = pltpu.SemaphoreType.DMA
    scratch = [
        pltpu.VMEM((2, slots, cells, channels), BF16),
        pltpu.VMEM((2, slots, cells, out_channels), BF16),
        pltpu.VMEM((n, 2 * cols, rows), BF16),
        pltpu.VMEM((2 * cols, kernel_rows), F32),
        pltpu.VMEM((9 * 2 * cols, channels), BF16),
        pltpu.VMEM((BLOCK, owned * cells, channels), BF16),
        pltpu.VMEM((BLOCK, padded, width), BF16),
        pltpu.VMEM((CHIPS, padded, width), BF16),
        pltpu.VMEM((9 * 2 * cols, width), F32),
        pltpu.VMEM((3 * cols, width), F32),
        pltpu.VMEM((3 * cols, width), F32),
        pltpu.VMEM((3 * cols, width), F32),
        pltpu.VMEM((9 * cols, channels), F32),
        pltpu.VMEM((n, up(cols * rows // LANES, 16), LANES), BF16),
        pltpu.VMEM((n, up(cols * rows // LANES, 16), LANES), BF16),
    ] + [sem] * 6 + [sem((9,))] * 2 + [sem] * 4
    turned = pl.pallas_call(
        functools.partial(kernel, n, 1.0 / (owned * n)),
        out_shape=jax.ShapeDtypeStruct((out_channels, rows), F32),
        in_specs=[smem] + [vmem] * 4,
        out_specs=vmem,
        scratch_shapes=scratch,
        compiler_params=pltpu.CompilerParams(
            collective_id=0, has_side_effects=True, vmem_limit_bytes=56 * 2**20
        ),
    )(
        table.reshape(3 * CHIPS * pair),
        latents.reshape(slots, cells, channels),
        targets.reshape(slots, cells, out_channels),
        both,
        mask,
    )
    return turned[:, :share].T


def solution(mesh):
    return jax.shard_map(
        per_device,
        mesh=mesh,
        in_specs=(
            P(("groups", "dp"), None, None, None),
            P(("groups", "dp"), None, None, None),
            P("groups"),
            P("groups"),
            P("groups"),
            P("dp", None),
            P(("groups", "dp"), None),
        ),
        out_specs=P(("groups", "dp"), None),
        check_vma=False,
    )
```
